512 devices in a mesh: sweep: 8 (over z_lo, core), recv: 64 (over x, y, z_hi).
Axes of the slice: x: 4, y: 8, z: 8 (z_hi: 2, z_lo: 4; z = z_hi * 4 + z_lo), core: 2. Of those that a mesh axis runs over, the one named last changes fastest.
Arguments:
- records: bfloat16 [16, 4096, 4096], P('sweep', 'recv'), may hold values from -6 to 6
- pilots: bfloat16 [16, 3968], replicated, may hold values from -0.09375 to 0.09375
- hadamard: int32 [16, 16], replicated, may hold values from -1 to 1, as said below
- code_vibrator: int32 [16], replicated, may hold values from 0 to 15, each once
- owner_map: int32 [4096], P('recv'), may hold values from 0 to 15
- live_mask: int32 [4096], P('recv'), may hold values 0 or 1
- filters: bfloat16 [16, 128, 128], P('sweep'), may hold values from -0.5 to 0.5
- targets: bfloat16 [16, 4096, 128], P('sweep', 'recv'), may hold values from -6 to 6
Outputs:
- responses: float32 [16, 4096, 128], P('sweep', 'recv')
- gradient: float32 [16, 128, 128], P('sweep', 'recv')
The draws below stay inside these ranges and needn't reach their ends.
Inputs may be any that keep to these rules, and one draw needn't show every extreme that they name: hadamard transposed times hadamard is 16 times the identity. `code_vibrator`: every vibrator belongs to exactly one code.
All inputs are finite; a program needn't handle non-finite values. No bound on the sum of `live_mask` on one device may be relied on, other than what follows from the above.
Results may differ from the reference program's by a relative error of at most 0.0085.
Values may be sent and summed in bfloat16 or wider, within the bound.
A program may use at most 64 MiB of HBM per device.

```python
import math
import jax
import jax.numpy as jnp
from jax import lax

CODES = 16
NT = 4096
NLAG = 128
LP = 3968
RECEIVERS = 4096


def draw_hadamard(key, part):
    subkeys = jax.random.split(jax.random.fold_in(key, 71), 3)
    indices = jnp.arange(CODES, dtype=jnp.int32)
    common_bits = indices[:, None] & indices[None, :]
    parity = jnp.zeros((CODES, CODES), jnp.int32)
    for bit_pos in range(CODES.bit_length() - 1):
        parity = parity + (common_bits >> bit_pos & 1)
    sylvester = 1 - 2 * (parity % 2)
    row_signs = 2 * jax.random.randint(subkeys[0], (CODES,), 0, 2) - 1
    col_signs = 2 * jax.random.randint(subkeys[1], (CODES,), 0, 2) - 1
    row_order = jax.random.permutation(subkeys[2], CODES)
    signed = sylvester[row_order] * row_signs[:, None] * col_signs[None, :]
    return signed.astype(jnp.int32)


def place_ends(array, key, smallest, top_value):
    longest = array.shape.index(max(array.shape))
    spots = []
    for shift in (0, 1):
        where = [jax.random.randint(jax.random.fold_in(key, axis), (), 0, length) for axis, length in enumerate(array.shape)]
        where[longest] = (where[longest] + shift) % array.shape[longest]
        spots.append(tuple(where))
    return array.at[spots[0]].set(smallest).at[spots[1]].set(top_value)


def block_levels(key, extent, cuts, least, high):
    def one(position, blocks):
        draws = jax.random.uniform(jax.random.fold_in(jax.random.fold_in(key, 6), position), (blocks,), jnp.float32, least / len(cuts), high / len(cuts))
        return jnp.repeat(jnp.exp(draws), extent[position] // blocks).reshape((-1,) + (1,) * (len(extent) - position - 1))

    loudness = one(*cuts[0])
    for cut in cuts[1:]:
        loudness = loudness * one(*cut)
    return loudness


def scatter_about(rng, shape, spread, most, cuts=(), held_as=jnp.bfloat16):
    factor_of = block_levels(rng, shape, cuts, -0.22, 0.18) if cuts else 1.0
    drawn = jax.random.normal(rng, shape, jnp.float32) * spread * factor_of
    return jnp.minimum(jnp.maximum(drawn, -most), most).astype(held_as)


def setup_inputs(seed: int = 0) -> dict:
    splits = jax.random.split(jax.random.key(seed), 9)
    records = scatter_about(splits[0], (CODES, RECEIVERS, NT), 1.0, 6.0, ((0, 8), (1, 64)))
    pilots = scatter_about(splits[1], (CODES, LP), LP ** -0.5, 0.09375)
    hadamard = draw_hadamard(jax.random.fold_in(splits[8], 71), 0)
    code_vibrator = jax.random.permutation(splits[3], CODES).astype(jnp.int32)
    owner_map = place_ends(jax.random.randint(splits[4], (RECEIVERS,), 0, CODES), jax.random.fold_in(splits[4], 1), 0, CODES - 1).astype(jnp.int32)
    live_mask = place_ends((jax.random.randint(splits[5], (RECEIVERS,), 0, 8) < 7).astype(jnp.int32), jax.random.fold_in(splits[5], 1), 0, 1)
    filters = scatter_about(splits[6], (CODES, NLAG, NLAG), NLAG ** -0.5, 0.5, ((0, 8),))
    targets = scatter_about(splits[7], (CODES, RECEIVERS, NLAG), 1.0, 6.0, ((0, 8), (1, 64)))
    return dict(records=records, pilots=pilots, hadamard=hadamard, code_vibrator=code_vibrator, owner_map=owner_map, live_mask=live_mask, filters=filters, targets=targets)


def toeplitz(sweep_pilot):
    padding = jnp.zeros((NT + 1 - sweep_pilot.shape[0],), sweep_pilot.dtype)
    extended = jnp.concatenate([sweep_pilot, padding])
    return jnp.tile(extended, NLAG)[:NLAG * NT].reshape(NLAG, NT)

def reference(records, pilots, hadamard, code_vibrator, owner_map, live_mask, filters, targets):
    onehot = (code_vibrator[:, None] == jnp.arange(CODES, dtype=jnp.int32)[None, :]).astype(jnp.float32)
    code_pilot = jnp.dot(onehot, pilots.astype(jnp.float32), precision=lax.Precision.HIGHEST)
    sign_table = hadamard.astype(jnp.float32)
    code_norm = 1.0 / math.sqrt(CODES)

    def per_code(operands):
        sign_col, sweep_pilot = operands
        combined = jnp.zeros((RECEIVERS, NT), jnp.float32)
        for sweep_index in range(CODES):
            combined = combined + sign_col[sweep_index] * records[sweep_index].astype(jnp.float32)
        toe_rows = toeplitz(sweep_pilot)
        lagged = lax.dot_general(combined, toe_rows, (((1,), (1,)), ((), ())), precision=lax.Precision.HIGHEST, preferred_element_type=jnp.float32)
        return code_norm * lagged
    decoded = lax.map(per_code, (sign_table.T, code_pilot))
    decoded_b = decoded.astype(jnp.bfloat16)
    dec_wide = decoded_b.astype(jnp.float32)
    responses = jnp.einsum('crl,clm->crm', dec_wide, filters.astype(jnp.float32), precision=lax.Precision.HIGHEST)
    owned = (owner_map[None, :] == code_vibrator[:, None]).astype(jnp.float32)
    weight = live_mask.astype(jnp.float32)[None, :] * (0.25 + owned)
    residual = (weight[:, :, None] * (responses - targets.astype(jnp.float32))).astype(jnp.bfloat16)
    gradient = jnp.einsum('crl,crm->clm', dec_wide, residual.astype(jnp.float32), precision=lax.Precision.HIGHEST)
    gradient = gradient * (1.0 / math.sqrt(RECEIVERS))
    return (responses, gradient)
```

```python
import functools
import math

import jax
import jax.numpy as jnp
from jax import lax
from jax.experimental import pallas as pl
from jax.experimental.pallas import tpu as pltpu
from jax.sharding import PartitionSpec as P

BF = jnp.bfloat16
F32 = jnp.float32
FINE = 16
LANES = 128


def kernel(
    ns, nr,
    rec_h, pil_h, had_h, cv_h, own_h, live_h, fil_h, tgt_h,
    resp_h, grad_h,
    rec, pil, had, cv, own, live, fil, tgt,
    rect, wmat, xs, sb, rb, wgt, resp, gs, ch, gb, gout,
    in_sem, s1_send, s1_recv, s2_send, s2_recv, out_sem,
):
    me = lax.axis_index("sweep")
    mr = lax.axis_index("recv")
    held, chans, samples = rec.shape
    codes, plen = pil.shape
    lags = fil.shape[1]
    owned = fil.shape[0]
    coarse = lags // FINE
    pairs = coarse // 2
    rows = lags // nr

    pairs_in = [
        (pil_h, pil), (cv_h, cv), (rec_h, rec), (had_h, had),
        (own_h, own), (live_h, live), (fil_h, fil), (tgt_h, tgt),
    ]
    loads = [pltpu.make_async_copy(a, b, in_sem.at[i]) for i, (a, b) in enumerate(pairs_in)]
    for c in loads:
        c.start()
    l_pil, l_cv, l_rec, l_had, l_own, l_live, l_fil, l_tgt = loads

    barrier = pltpu.get_barrier_semaphore()
    for k in range(1, ns):
        pl.semaphore_signal(barrier, inc=1, device_id={"sweep": lax.rem(me + k, ns)},
                            device_id_type=pl.DeviceIdType.MESH)
    @pl.loop(1, nr)
    def _(k):
        pl.semaphore_signal(barrier, inc=1, device_id={"recv": lax.rem(mr + k, nr)},
                            device_id_type=pl.DeviceIdType.MESH)

    l_pil.wait()
    l_cv.wait()
    row = lax.broadcasted_iota(jnp.int32, (codes, codes), 0)
    col = lax.broadcasted_iota(jnp.int32, (codes, codes), 1)
    pick = jnp.zeros((codes, codes), jnp.int32)
    for q in range(codes):
        v = cv[lax.rem(owned * me + q, codes)]
        pick = jnp.where(row == q, v, pick)
    onehot = (pick == col).astype(F32).astype(BF)
    cp = jnp.dot(onehot, pil[...], preferred_element_type=F32)
    cp = jnp.concatenate([cp, jnp.zeros((codes, samples - plen), F32)], axis=1)
    for f in range(FINE):
        shifted = cp if f == 0 else pltpu.roll(cp, f, 1)
        wmat[f * codes:(f + 1) * codes, :] = shifted.astype(BF)

    l_rec.wait()
    for b in range(samples // LANES):
        blk = rec[:, :, b * LANES:(b + 1) * LANES].reshape(held * chans, LANES)
        rect[b * LANES:(b + 1) * LANES, :] = blk.T
    rect[samples:samples + LANES, :] = jnp.zeros((LANES, LANES), BF)

    l_had.wait()
    low = lax.broadcasted_iota(jnp.int32, (1, LANES), 1) < chans
    norm = 1.0 / math.sqrt(codes)
    coef = []
    for q in range(codes):
        c = lax.rem(owned * me + q, codes)
        h0 = had[held * me, c].astype(F32) * norm
        h1 = had[held * me + 1, c].astype(F32) * norm
        coef.append(jnp.where(low, h0, h1))

    l_own.wait()
    l_live.wait()
    own_t = jnp.broadcast_to(own[...].astype(F32), (LANES, chans)).T
    live_t = jnp.broadcast_to(live[...].astype(F32), (LANES, chans)).T
    for c in range(owned):
        v = cv[owned * me + c].astype(F32)
        wgt[c * chans:(c + 1) * chans, :] = live_t * jnp.where(own_t == v, 1.25, 0.25)

    pl.semaphore_wait(barrier, ns - 1 + nr - 1)

    def copy1(k, p):
        return pltpu.make_async_remote_copy(
            src_ref=sb.at[k, pl.ds(2 * FINE * p, 2 * FINE)],
            dst_ref=rb.at[k - 1, pl.ds(2 * FINE * p, 2 * FINE)],
            send_sem=s1_send.at[k - 1, p], recv_sem=s1_recv.at[k - 1, p],
            device_id={"sweep": lax.rem(me + k, ns)}, device_id_type=pl.DeviceIdType.MESH)

    for p in range(pairs):
        base = 2 * FINE * p
        rhs = jnp.concatenate(
            [rect[base:base + samples, :], rect[base + FINE:base + FINE + samples, :]], axis=1)
        acc = jnp.dot(wmat[...], rhs, preferred_element_type=F32)
        xs[p, 0] = acc[:, :LANES]
        xs[p, 1] = acc[:, LANES:]
        for kk in range(ns):
            k = (kk + 1) % ns
            for par in range(2):
                a = xs[p, par, pl.ds(2 * k, FINE, stride=codes), :] * coef[2 * k]
                b = xs[p, par, pl.ds(2 * k + 1, FINE, stride=codes), :] * coef[2 * k + 1]
                part = jnp.where(low, a, b) + pltpu.roll(jnp.where(low, b, a), chans, 1)
                lo = base + par * FINE
                sb[k, lo:lo + FINE, :] = part.astype(BF)
            if k:
                copy1(k, p).start()

    pieces = []
    for p in range(pairs):
        base = 2 * FINE * p
        tot = sb[0, base:base + 2 * FINE, :].astype(F32)
        for k in range(1, ns):
            copy1(k, p).wait_recv()
            tot = tot + rb[k - 1, base:base + 2 * FINE, :].astype(F32)
        pieces.append(tot)
    dec_t32 = jnp.concatenate(pieces, axis=0)
    dec_t = dec_t32.astype(BF)
    dec = dec_t.T
    l_fil.wait()
    l_tgt.wait()
    res = []
    rowid = lax.broadcasted_iota(jnp.int32, (owned * chans, 1), 0)
    for c in range(owned):
        r = jnp.dot(dec[c * chans:(c + 1) * chans, :], fil[c], preferred_element_type=F32)
        resp[c] = r
        res.append(wgt[c * chans:(c + 1) * chans, :] * (r - tgt[c].astype(F32)))
    out1 = pltpu.make_async_copy(resp, resp_h, out_sem.at[0])
    out1.start()
    zero = jnp.zeros((chans, LANES), BF)
    res2 = jnp.concatenate([
        jnp.concatenate([res[0].astype(BF), zero], axis=1),
        jnp.concatenate([zero, res[1].astype(BF)], axis=1)], axis=0)
    g = jnp.dot(dec_t, res2, preferred_element_type=F32)
    for c in range(owned):
        gs[c] = g[:, c * lags:(c + 1) * lags]
    parts = []
    for c in range(owned):
        for i in range(rows):
            parts.append(gs[c, pl.ds(i, nr, stride=rows), :])
    ch[...] = jnp.stack(parts, axis=1).astype(BF)

    def copy2(k):
        j = lax.rem(mr + k, nr)
        return pltpu.make_async_remote_copy(
            src_ref=ch.at[j], dst_ref=gb.at[k], send_sem=s2_send.at[0], recv_sem=s2_recv.at[0],
            device_id={"recv": j}, device_id_type=pl.DeviceIdType.MESH)

    @pl.loop(1, nr)
    def _(k):
        copy2(k).start()

    total = ch[mr].astype(F32)
    for p in range(pairs):
        for k in range(1, ns):
            copy1(k, p).wait_send()
    everything = gb.at[pl.ds(1, nr - 1)]
    pltpu.make_async_copy(everything, everything, s2_recv.at[0]).wait()
    total = total + jnp.sum(gb[pl.ds(1, nr - 1)].astype(F32), axis=0)
    factor = 1.0 / math.sqrt(chans * nr)
    for c in range(owned):
        gout[c] = total[c * rows:(c + 1) * rows, :] * factor
    out2 = pltpu.make_async_copy(gout, grad_h, out_sem.at[1])
    out2.start()
    sent = ch.at[pl.ds(0, nr - 1)]
    pltpu.make_async_copy(sent, sent, s2_send.at[0]).wait()
    out1.wait()
    out2.wait()


def solution(mesh):
    ns, nr = mesh.shape["sweep"], mesh.shape["recv"]

    def local(records, pilots, hadamard, code_vibrator, owner_map, live_mask, filters, targets):
        held, chans, samples = records.shape
        codes, plen = pilots.shape
        owned, lags, _ = filters.shape
        rows = lags // nr
        any_spec = pl.BlockSpec(memory_space=pltpu.HBM)
        vm = pltpu.VMEM
        return pl.pallas_call(
            functools.partial(kernel, ns, nr),
            out_shape=(
                jax.ShapeDtypeStruct((owned, chans, lags), F32),
                jax.ShapeDtypeStruct((owned, rows, lags), F32),
            ),
            in_specs=[any_spec] * 8,
            out_specs=(any_spec, any_spec),
            scratch_shapes=[
                vm((held, chans, samples), BF), vm((codes, plen), BF),
                pltpu.SMEM((codes, codes), jnp.int32), pltpu.SMEM((codes,), jnp.int32),
                vm((1, chans), jnp.int32), vm((1, chans), jnp.int32),
                vm((owned, lags, lags), BF), vm((owned, chans, lags), BF),
                vm((samples + LANES, LANES), BF), vm((FINE * codes, samples), BF),
                vm((lags // FINE // 2, 2, FINE * codes, LANES), F32),
                vm((ns, lags, LANES), BF), vm((ns - 1, lags, LANES), BF),
                vm((owned * chans, LANES), F32), vm((owned, chans, lags), F32),
                vm((owned, lags, lags), F32),
                vm((nr, owned * rows, lags), BF), vm((nr, owned * rows, lags), BF),
                vm((owned, rows, lags), F32),
                pltpu.SemaphoreType.DMA((8,)),
                pltpu.SemaphoreType.DMA((ns - 1, lags // FINE // 2)),
                pltpu.SemaphoreType.DMA((ns - 1, lags // FINE // 2)),
                pltpu.SemaphoreType.DMA((1,)), pltpu.SemaphoreType.DMA((1,)),
                pltpu.SemaphoreType.DMA((2,)),
            ],
            compiler_params=pltpu.CompilerParams(
                collective_id=0, has_side_effects=True, vmem_limit_bytes=64 * 1024 * 1024),
        )(records, pilots, hadamard, code_vibrator, owner_map.reshape(1, -1),
          live_mask.reshape(1, -1), filters, targets)

    in_specs = (
        P("sweep", "recv", None), P(), P(), P(), P("recv"), P("recv"),
        P("sweep", None, None), P("sweep", "recv", None),
    )
    out_specs = (P("sweep", "recv", None), P("sweep", "recv", None))
    return jax.shard_map(local, mesh=mesh, in_specs=in_specs, out_specs=out_specs, check_vma=False)
```

```python
import functools
import math

import jax
import jax.numpy as jnp
from jax import lax
from jax.experimental import pallas as pl
from jax.experimental.pallas import tpu as pltpu
from jax.sharding import PartitionSpec as P

BF = jnp.bfloat16
F32 = jnp.float32
FINE = 16
LANES = 128
GROUP = 2
PARTS = 4
MESH = pl.DeviceIdType.MESH


def cube(nr):
    return (4, 8, 2) if nr == 64 else (1, nr // 2, 2)


def kernel(
    ns, nr,
    rec_h, pil_h, had_h, cv_h, own_h, live_h, fil_h, tgt_h,
    resp, grad,
    rec, pil, had, cv, own, live, fil, tgt,
    rect, wmat, xs, sb, rb, wgt, gs, ch, gb,
    in_sem, rec_sem, sib_send, sib_recv, s1_send, s1_recv, s2_send, s2_recv, relay,
):
    me = lax.axis_index("sweep")
    mr = lax.axis_index("recv")
    _, held, half, samples = rec.shape
    chans = 2 * half
    codes, plen = pil.shape
    lags = fil.shape[1]
    owned = fil.shape[0]
    pairs = lags // FINE // 2
    rows = lags // nr
    nx, ny, nz = cube(nr)
    x, y, z = mr // (ny * nz), mr // nz % ny, mr % nz
    core = me % 2
    bits = (me // 4, me // 2 % 2, core)

    def mate(k):
        a, b, c = [1 - v if k >> (2 - i) & 1 else v for i, v in enumerate(bits)]
        return a * 4 + b * 2 + c

    def at(dx, dy, dz):
        return ((x + dx) % nx * ny + (y + dy) % ny) * nz + (z + dz) % nz

    sib = mate(1)
    order = [6, 7, 4, 5, 2, 3, 1]

    part = samples // PARTS
    mine = pl.ds(pl.multiple_of(core * half, half), half)
    theirs = pl.ds(pl.multiple_of((1 - core) * half, half), half)
    small = [(pil_h, pil), (cv_h, cv), (had_h, had), (own_h, own), (live_h, live), (fil_h, fil), (tgt_h, tgt)]
    loads = [pltpu.make_async_copy(a, b, in_sem.at[i]) for i, (a, b) in enumerate(small)]
    own_rec = [
        pltpu.make_async_copy(
            rec_h.at[:, mine, pl.ds(i * part, part)], rec.at[0, :, :, pl.ds(i * part, part)], rec_sem.at[i])
        for i in range(PARTS)
    ]
    l_pil, l_cv, l_had, l_own, l_live, l_fil, l_tgt = loads
    l_pil.start()
    l_cv.start()
    for c in own_rec:
        c.start()
    for c in loads[2:]:
        c.start()

    barrier = pltpu.get_barrier_semaphore()
    greet = [{"sweep": mate(k)} for k in [1] + order[:-1]]
    ys = [{"recv": at(0, d, 0)} for d in range(1, ny)]
    zs = [{"recv": at(0, 0, d)} for d in range(1, nz)]
    greet += ys + zs + [{"recv": at(d, 0, 0)} for d in range(1, nx)]
    for d in greet:
        pl.semaphore_signal(barrier, inc=1, device_id=d, device_id_type=MESH)

    l_pil.wait()
    l_cv.wait()
    slot_code = [owned * mate(k) + i for k in range(ns) for i in range(owned)]
    row = lax.broadcasted_iota(jnp.int32, (codes, codes), 0)
    col = lax.broadcasted_iota(jnp.int32, (codes, codes), 1)
    pick = jnp.zeros((codes, codes), jnp.int32)
    for q in range(codes):
        pick = jnp.where(row == q, cv[slot_code[q]], pick)
    onehot = (pick == col).astype(F32).astype(BF)
    cp = jnp.dot(onehot, pil[...], preferred_element_type=F32)
    cp = jnp.concatenate([cp, jnp.zeros((codes, samples - plen), F32)], axis=1)
    for f in range(FINE):
        shifted = cp if f == 0 else pltpu.roll(cp, f, 1)
        wmat[f * codes:(f + 1) * codes, :] = shifted.astype(BF)

    pl.semaphore_wait(barrier, len(greet))
    trade = [
        pltpu.make_async_remote_copy(
            src_ref=rec_h.at[:, theirs, pl.ds(i * part, part)],
            dst_ref=rec.at[1, :, :, pl.ds(i * part, part)],
            send_sem=sib_send.at[i], recv_sem=sib_recv.at[i],
            device_id={"sweep": sib}, device_id_type=MESH)
        for i in range(PARTS)
    ]
    for c in trade:
        c.start()
    for d in ys:
        pl.semaphore_signal(relay.at[0], inc=1, device_id=d, device_id_type=MESH)

    lane = lax.broadcasted_iota(jnp.int32, (1, LANES), 1)
    group = lane // half
    l_had.wait()
    norm = 1.0 / math.sqrt(codes)
    sweeps = [held * me + i for i in range(held)] + [held * sib + i for i in range(held)]
    coef = []
    for q in range(codes):
        v = jnp.zeros((1, LANES), F32)
        for g, s in enumerate(sweeps):
            v = jnp.where(group == g, had[s, slot_code[q]].astype(F32) * norm, v)
        coef.append(v)
    l_own.wait()
    l_live.wait()
    own_t = jnp.broadcast_to(own[...].astype(F32), (LANES, chans)).T
    live_t = jnp.broadcast_to(live[...].astype(F32), (LANES, chans)).T
    for c in range(owned):
        v = cv[owned * me + c].astype(F32)
        wgt[c * chans:(c + 1) * chans, :] = live_t * jnp.where(own_t == v, 1.25, 0.25)

    rect[samples:samples + LANES, :] = jnp.zeros((LANES, LANES), BF)
    for i in range(PARTS):
        own_rec[i].wait()
        trade[i].wait_recv()
        for b in range(i * part // LANES, (i + 1) * part // LANES):
            blk = rec[:, :, :, b * LANES:(b + 1) * LANES].reshape(2 * held * half, LANES)
            rect[b * LANES:(b + 1) * LANES, :] = blk.T

    def copy1(k, p):
        return pltpu.make_async_remote_copy(
            src_ref=sb.at[k, pl.ds(p * GROUP, GROUP)], dst_ref=rb.at[k - 1, pl.ds(p * GROUP, GROUP)],
            send_sem=s1_send.at[k - 1, p], recv_sem=s1_recv.at[k - 1, p],
            device_id={"sweep": mate(k)}, device_id_type=MESH)

    low = group < 2
    outer = (group == 0) | (group == 3)
    even = group % 2 == 0
    def correlate(p):
        base = 2 * FINE * p
        rhs = jnp.concatenate(
            [rect[base:base + samples, :], rect[base + FINE:base + FINE + samples, :]], axis=1)
        acc = jnp.dot(wmat[...], rhs, preferred_element_type=F32)
        xs[p, 0] = acc[:, :LANES]
        xs[p, 1] = acc[:, LANES:]

    def decode(p):
        for k in order + [0]:
            a0, b0, a1, b1 = [
                xs[p, par, pl.ds(2 * k + i, FINE, stride=codes), :] * coef[2 * k + i]
                for par in range(2) for i in range(2)
            ]
            u = jnp.where(low, b0, b1) + pltpu.roll(jnp.where(low, b1, b0), 2 * half, 1)
            v = jnp.where(outer, a0, a1) + pltpu.roll(jnp.where(outer, a1, a0), 2 * half, 1)
            t = jnp.where(even, v, u) + pltpu.roll(jnp.where(even, u, v), half, 1)
            sb[k, p] = t.astype(BF)

    for p in range(pairs):
        correlate(p)
        decode(p)
        if p % GROUP == GROUP - 1:
            for k in order:
                copy1(k, p // GROUP).start()

    pl.semaphore_wait(relay.at[0], ny - 1)
    for d in zs:
        pl.semaphore_signal(relay.at[1], inc=1, device_id=d, device_id_type=MESH)

    first = jnp.full((FINE, LANES), core, jnp.int32) == 0
    pieces = []
    for p in range(pairs):
        if p % GROUP == 0:
            for k in order:
                copy1(k, p // GROUP).wait_recv()
        here = sb[0, p].astype(F32)
        for k in (6, 4, 2):
            here = here + rb[k - 1, p].astype(F32)
        there = None
        for k in (7, 5, 3, 1):
            v = rb[k - 1, p].astype(F32)
            there = v if there is None else there + v
        h0 = jnp.where(first, here, there)
        h1 = jnp.where(first, there, here)
        pieces.append(jnp.where(low, h0, pltpu.roll(h1, 2 * half, 1)))
        pieces.append(jnp.where(low, pltpu.roll(h0, 2 * half, 1), h1))
    dec_t = jnp.concatenate(pieces, axis=0).astype(BF)
    dec = dec_t.T
    l_fil.wait()
    l_tgt.wait()
    res = []
    for c in range(owned):
        lhs = jnp.concatenate([dec[(h * owned + c) * half:(h * owned + c + 1) * half, :] for h in range(2)], axis=0)
        r = jnp.dot(lhs, fil[c], preferred_element_type=F32)
        resp[c] = r
        res.append((wgt[c * chans:(c + 1) * chans, :] * (r - tgt[c].astype(F32))).astype(BF))
    zero = jnp.zeros((half, lags), BF)
    blocks = []
    for h in range(2):
        for c in range(owned):
            blocks.append(jnp.concatenate(
                [res[c][h * half:(h + 1) * half, :] if e == c else zero for e in range(owned)], axis=1))
    g = jnp.dot(dec_t, jnp.concatenate(blocks, axis=0), preferred_element_type=F32)
    for c in range(owned):
        gs[c] = g[:, c * lags:(c + 1) * lags]
    ch[...] = jnp.stack(
        [gs[c, pl.ds(i, nr, stride=rows), :] for c in range(owned) for i in range(rows)], axis=1).astype(BF)

    steps = [(dx, dy, dz) for dx in range(nx) for dy in range(ny) for dz in range(nz)]
    steps.sort(key=lambda s: -(min(s[0], nx - s[0]) + min(s[1], ny - s[1]) + 4 * s[2]))
    pl.semaphore_wait(relay.at[1], nz - 1)
    for n, s in enumerate(steps[:-1]):
        j = at(*s)
        pltpu.make_async_remote_copy(
            src_ref=ch.at[j], dst_ref=gb.at[n], send_sem=s2_send.at[0], recv_sem=s2_recv.at[0],
            device_id={"recv": j}, device_id_type=MESH).start()

    total = ch[mr].astype(F32)
    for c in trade:
        c.wait_send()
    for p in range(pairs // GROUP):
        for k in order:
            copy1(k, p).wait_send()
    sent = ch.at[pl.ds(0, nr - 1)]
    pltpu.make_async_copy(sent, sent, s2_send.at[0]).wait()
    pltpu.make_async_copy(gb, gb, s2_recv.at[0]).wait()
    total = total + jnp.sum(gb[...].astype(F32), axis=0)
    factor = 1.0 / math.sqrt(chans * nr)
    for c in range(owned):
        grad[c] = total[c * rows:(c + 1) * rows, :] * factor


def solution(mesh):
    ns, nr = mesh.shape["sweep"], mesh.shape["recv"]

    def local(records, pilots, hadamard, code_vibrator, owner_map, live_mask, filters, targets):
        held, chans, samples = records.shape
        codes, plen = pilots.shape
        owned, lags, _ = filters.shape
        rows = lags // nr
        pairs = lags // FINE // 2
        vm = pltpu.VMEM
        dma = pltpu.SemaphoreType.DMA
        operands = (records, pilots, hadamard, code_vibrator, owner_map.reshape(1, -1),
                    live_mask.reshape(1, -1), filters, targets)
        return pl.pallas_call(
            functools.partial(kernel, ns, nr),
            out_shape=(vm((owned, chans, lags), F32), vm((owned, rows, lags), F32)),
            in_specs=[pl.BlockSpec(memory_space=pltpu.HBM)] * 8,
            out_specs=(pl.BlockSpec(memory_space=vm),) * 2,
            scratch_shapes=[
                vm((2, held, chans // 2, samples), BF), vm((codes, plen), BF),
                pltpu.SMEM((codes, codes), jnp.int32), pltpu.SMEM((codes,), jnp.int32),
                vm((1, chans), jnp.int32), vm((1, chans), jnp.int32),
                vm((owned, lags, lags), BF), vm((owned, chans, lags), BF),
                vm((samples + LANES, LANES), BF), vm((FINE * codes, samples), BF),
                vm((pairs, 2, FINE * codes, LANES), F32),
                vm((ns, pairs, FINE, LANES), BF), vm((ns - 1, pairs, FINE, LANES), BF),
                vm((owned * chans, lags), F32), vm((owned, lags, lags), F32),
                vm((nr, owned * rows, lags), BF), vm((nr - 1, owned * rows, lags), BF),
                dma((7,)), dma((PARTS,)), dma((PARTS,)), dma((PARTS,)),
                dma((ns - 1, pairs // GROUP)), dma((ns - 1, pairs // GROUP)), dma((1,)), dma((1,)),
                pltpu.SemaphoreType.REGULAR((2,)),
            ],
            compiler_params=pltpu.CompilerParams(
                collective_id=0, has_side_effects=True, vmem_limit_bytes=40 * 1024 * 1024),
        )(*[pltpu.with_memory_space_constraint(a, pltpu.HBM) for a in operands])

    in_specs = (
        P("sweep", "recv", None), P(), P(), P(), P("recv"), P("recv"),
        P("sweep", None, None), P("sweep", "recv", None),
    )
    out_specs = (P("sweep", "recv", None), P("sweep", "recv", None))
    return jax.shard_map(local, mesh=mesh, in_specs=in_specs, out_specs=out_specs, check_vma=False)
```

```python
import functools
import math

import jax
import jax.numpy as jnp
from jax import lax
from jax.experimental import pallas as pl
from jax.experimental.pallas import tpu as pltpu
from jax.sharding import PartitionSpec as P

BF = jnp.bfloat16
F32 = jnp.float32
FINE = 32
LANES = 128
SIDES = 2
PARTS = 4
MESH = pl.DeviceIdType.MESH


def cube(nr):
    return (4, 8, 2) if nr == 64 else (1, nr // 2, 2)


def kernel(
    ns, nr,
    rec_h, pil_h, had_h, cv_h, own_h, live_h, fil_h, tgt_h,
    resp, grad,
    rec, pil, had, cv, own, live, fil, tgt,
    rect, wmat, xs, sb, rb, wgt, gs, ch, gb,
    in_sem, rec_sem, sib_send, sib_recv, s1_send, s1_recv, s2_send, s2_recv, pair, relay,
):
    me = lax.axis_index("sweep")
    mr = lax.axis_index("recv")
    _, held, half, samples = rec.shape
    chans = 2 * half
    codes, plen = pil.shape
    lags = fil.shape[1]
    owned = fil.shape[0]
    pairs = lags // FINE // 2
    rows = lags // nr
    nx, ny, nz = cube(nr)
    x, y, z = mr // (ny * nz), mr // nz % ny, mr % nz
    core = me % 2
    bits = (me // 4, me // 2 % 2, core)

    def mate(k):
        a, b, c = [1 - v if k >> (2 - i) & 1 else v for i, v in enumerate(bits)]
        return a * 4 + b * 2 + c

    def at(dx, dy, dz):
        return ((x + dx) % nx * ny + (y + dy) % ny) * nz + (z + dz) % nz

    sib = mate(1)
    order = [[6, 7, 4, 5], [2, 3, 1]]
    ranks = ns // SIDES
    slots = codes // SIDES

    part = samples // PARTS
    mine = pl.ds(pl.multiple_of(core * half, half), half)
    theirs = pl.ds(pl.multiple_of((1 - core) * half, half), half)
    small = [(pil_h, pil), (cv_h, cv), (had_h, had), (own_h, own), (live_h, live), (fil_h, fil), (tgt_h, tgt)]
    loads = [pltpu.make_async_copy(a, b, in_sem.at[i]) for i, (a, b) in enumerate(small)]
    own_rec = [
        pltpu.make_async_copy(
            rec_h.at[:, mine, pl.ds(i * part, part)], rec.at[0, :, :, pl.ds(i * part, part)], rec_sem.at[i])
        for i in range(PARTS)
    ]
    l_pil, l_cv, l_had, l_own, l_live, l_fil, l_tgt = loads
    l_pil.start()
    l_cv.start()
    for c in own_rec:
        c.start()
    for c in loads[2:]:
        c.start()

    barrier = pltpu.get_barrier_semaphore()
    ys = [{"recv": at(0, d, 0)} for d in range(1, ny)]
    zs = [{"recv": at(0, 0, d)} for d in range(1, nz)]
    greet = [{"sweep": mate(k)} for k in range(2, ns, 2)]
    greet += ys + zs + [{"recv": at(d, 0, 0)} for d in range(1, nx)]

    def tell(sem, device):
        pl.semaphore_signal(sem, inc=1, device_id=device, device_id_type=MESH)

    @pl.when(core == 1)
    def _():
        tell(barrier, {"sweep": sib})

    @pl.when(core == 0)
    def _():
        pl.semaphore_wait(barrier, 1)
        tell(pair.at[0], {"sweep": sib})

    @pl.when(core == 1)
    def _():
        pl.semaphore_wait(pair.at[0], 1)

    trade = [
        pltpu.make_async_remote_copy(
            src_ref=rec_h.at[:, theirs, pl.ds(i * part, part)],
            dst_ref=rec.at[1, :, :, pl.ds(i * part, part)],
            send_sem=sib_send.at[i], recv_sem=sib_recv.at[i],
            device_id={"sweep": sib}, device_id_type=MESH)
        for i in range(PARTS)
    ]
    for c in trade:
        c.start()

    @pl.when(core == 1)
    def _():
        for d in greet:
            tell(barrier, d)

    l_pil.wait()
    l_cv.wait()
    slot_code = [owned * mate(k) + i for k in range(ns) for i in range(owned)]
    row = lax.broadcasted_iota(jnp.int32, (codes, codes), 0)
    col = lax.broadcasted_iota(jnp.int32, (codes, codes), 1)
    pick = jnp.zeros((codes, codes), jnp.int32)
    for q in range(codes):
        pick = jnp.where(row == q, cv[slot_code[q]], pick)
    onehot = (pick == col).astype(F32).astype(BF)
    cp = jnp.dot(onehot, pil[...], preferred_element_type=F32)
    cp = jnp.concatenate([cp, jnp.zeros((codes, samples - plen), F32)], axis=1)
    for f in range(0, FINE, 2):
        a = cp if f == 0 else pltpu.roll(cp, f, 1)
        b = pltpu.roll(cp, f + 1, 1)
        for g in range(SIDES):
            both = jnp.concatenate([a[g * slots:(g + 1) * slots], b[g * slots:(g + 1) * slots]], axis=0)
            wmat[g, f * slots:(f + 2) * slots, :] = both.astype(BF)

    lane = lax.broadcasted_iota(jnp.int32, (1, LANES), 1)
    group = lane // half
    l_had.wait()
    norm = 1.0 / math.sqrt(codes)
    sweeps = [held * me + i for i in range(held)] + [held * sib + i for i in range(held)]
    coef = []
    for q in range(codes):
        v = jnp.zeros((1, LANES), F32)
        for g, s in enumerate(sweeps):
            v = jnp.where(group == g, had[s, slot_code[q]].astype(F32) * norm, v)
        coef.append(v)
    l_own.wait()
    l_live.wait()
    own_t = jnp.broadcast_to(own[...].astype(F32), (LANES, chans)).T
    live_t = jnp.broadcast_to(live[...].astype(F32), (LANES, chans)).T
    for c in range(owned):
        v = cv[owned * me + c].astype(F32)
        wgt[c * chans:(c + 1) * chans, :] = live_t * jnp.where(own_t == v, 1.25, 0.25)

    rect[samples:samples + LANES, :] = jnp.zeros((LANES, LANES), BF)
    for i in range(PARTS):
        own_rec[i].wait()
        trade[i].wait_recv()
        for b in range(i * part // LANES, (i + 1) * part // LANES):
            blk = rec[:, :, :, b * LANES:(b + 1) * LANES].reshape(2 * held * half, LANES)
            rect[b * LANES:(b + 1) * LANES, :] = blk.T

    def copy1(k):
        return pltpu.make_async_remote_copy(
            src_ref=sb.at[k], dst_ref=rb.at[k - 1],
            send_sem=s1_send.at[k - 1], recv_sem=s1_recv.at[k - 1],
            device_id={"sweep": mate(k)}, device_id_type=MESH)

    low = group < 2
    outer = (group == 0) | (group == 3)
    even = group % 2 == 0
    def correlate(g, p):
        base = 2 * FINE * p
        rhs = jnp.concatenate(
            [rect[base:base + samples, :], rect[base + FINE:base + FINE + samples, :]], axis=1)
        acc = jnp.dot(wmat[g], rhs, preferred_element_type=F32)
        xs[g, p, 0] = acc[:, :LANES]
        xs[g, p, 1] = acc[:, LANES:]

    def decode(g, p, k):
        q = owned * (k % ranks)
        a0, b0, a1, b1 = [
            xs[g, p, par, pl.ds(q + i, FINE, stride=slots), :] * coef[owned * k + i]
            for par in range(2) for i in range(owned)
        ]
        u = jnp.where(low, b0, b1) + pltpu.roll(jnp.where(low, b1, b0), 2 * half, 1)
        v = jnp.where(outer, a0, a1) + pltpu.roll(jnp.where(outer, a1, a0), 2 * half, 1)
        t = jnp.where(even, v, u) + pltpu.roll(jnp.where(even, u, v), half, 1)
        sb[k, p] = t.astype(BF)

    for g in (1, 0):
        for p in range(pairs):
            correlate(g, p)
            for k in range(g * ranks, (g + 1) * ranks):
                decode(g, p, k)
        if g == 1:
            @pl.when(core == 1)
            def _():
                pl.semaphore_wait(barrier, len(greet))
                tell(pair.at[1], {"sweep": sib})

            @pl.when(core == 0)
            def _():
                pl.semaphore_wait(pair.at[1], 1)

        for k in order[1 - g]:
            copy1(k).start()
        if g == 1:
            for d in ys:
                tell(relay.at[0], d)

    pl.semaphore_wait(relay.at[0], ny - 1)
    for d in zs:
        tell(relay.at[1], d)

    first = jnp.full((FINE, LANES), core, jnp.int32) == 0
    pieces = []
    for ks in order:
        for k in ks:
            copy1(k).wait_recv()
    for p in range(pairs):
        here = sb[0, p].astype(F32)
        for k in (6, 4, 2):
            here = here + rb[k - 1, p].astype(F32)
        there = rb[6, p].astype(F32)
        for k in (5, 3, 1):
            there = there + rb[k - 1, p].astype(F32)
        h0 = jnp.where(first, here, there)
        h1 = jnp.where(first, there, here)
        pieces.append(jnp.where(low, h0, pltpu.roll(h1, 2 * half, 1)))
        pieces.append(jnp.where(low, pltpu.roll(h0, 2 * half, 1), h1))
    dec_t = jnp.concatenate(pieces, axis=0).astype(BF)
    dec = dec_t.T
    l_fil.wait()
    l_tgt.wait()
    res = []
    for c in range(owned):
        lhs = jnp.concatenate([dec[(h * owned + c) * half:(h * owned + c + 1) * half, :] for h in range(2)], axis=0)
        r = jnp.dot(lhs, fil[c], preferred_element_type=F32)
        resp[c] = r
        res.append((wgt[c * chans:(c + 1) * chans, :] * (r - tgt[c].astype(F32))).astype(BF))
    zero = jnp.zeros((half, lags), BF)
    blocks = []
    for h in range(2):
        for c in range(owned):
            blocks.append(jnp.concatenate(
                [res[c][h * half:(h + 1) * half, :] if e == c else zero for e in range(owned)], axis=1))
    g = jnp.dot(dec_t, jnp.concatenate(blocks, axis=0), preferred_element_type=F32)
    for c in range(owned):
        gs[c] = g[:, c * lags:(c + 1) * lags]
    ch[...] = jnp.stack(
        [gs[c, pl.ds(i, nr, stride=rows), :] for c in range(owned) for i in range(rows)], axis=1).astype(BF)

    steps = [(dx, dy, dz) for dx in range(nx) for dy in range(ny) for dz in range(nz)]
    steps.sort(key=lambda s: -(min(s[0], nx - s[0]) + min(s[1], ny - s[1]) + 4 * s[2]))
    pl.semaphore_wait(relay.at[1], nz - 1)
    for n, s in enumerate(steps[:-1]):
        j = at(*s)
        pltpu.make_async_remote_copy(
            src_ref=ch.at[j], dst_ref=gb.at[n], send_sem=s2_send.at[0], recv_sem=s2_recv.at[0],
            device_id={"recv": j}, device_id_type=MESH).start()

    total = ch[mr].astype(F32)
    for c in trade:
        c.wait_send()
    for ks in order:
        for k in ks:
            copy1(k).wait_send()
    sent = ch.at[pl.ds(0, nr - 1)]
    pltpu.make_async_copy(sent, sent, s2_send.at[0]).wait()
    pltpu.make_async_copy(gb, gb, s2_recv.at[0]).wait()
    total = total + jnp.sum(gb[...].astype(F32), axis=0)
    factor = 1.0 / math.sqrt(chans * nr)
    for c in range(owned):
        grad[c] = total[c * rows:(c + 1) * rows, :] * factor


def deliver(resp_v, grad_v, resp_h, grad_h, sem):
    outs = [pltpu.make_async_copy(resp_v, resp_h, sem.at[0]), pltpu.make_async_copy(grad_v, grad_h, sem.at[1])]
    for c in outs:
        c.start()
    for c in outs:
        c.wait()


def solution(mesh):
    ns, nr = mesh.shape["sweep"], mesh.shape["recv"]

    def local(records, pilots, hadamard, code_vibrator, owner_map, live_mask, filters, targets):
        held, chans, samples = records.shape
        codes, plen = pilots.shape
        owned, lags, _ = filters.shape
        rows = lags // nr
        pairs = lags // FINE // 2
        vm = pltpu.VMEM
        dma = pltpu.SemaphoreType.DMA
        operands = (records, pilots, hadamard, code_vibrator, owner_map.reshape(1, -1),
                    live_mask.reshape(1, -1), filters, targets)
        outs = pl.pallas_call(
            functools.partial(kernel, ns, nr),
            out_shape=(vm((owned, chans, lags), F32), vm((owned, rows, lags), F32)),
            in_specs=[pl.BlockSpec(memory_space=pltpu.HBM)] * 8,
            out_specs=(pl.BlockSpec(memory_space=vm),) * 2,
            scratch_shapes=[
                vm((2, held, chans // 2, samples), BF), vm((codes, plen), BF),
                pltpu.SMEM((codes, codes), jnp.int32), pltpu.SMEM((codes,), jnp.int32),
                vm((1, chans), jnp.int32), vm((1, chans), jnp.int32),
                vm((owned, lags, lags), BF), vm((owned, chans, lags), BF),
                vm((samples + LANES, LANES), BF), vm((SIDES, FINE * codes // SIDES, samples), BF),
                vm((SIDES, pairs, 2, FINE * codes // SIDES, LANES), F32),
                vm((ns, pairs, FINE, LANES), BF), vm((ns - 1, pairs, FINE, LANES), BF),
                vm((owned * chans, lags), F32), vm((owned, lags, lags), F32),
                vm((nr, owned * rows, lags), BF), vm((nr - 1, owned * rows, lags), BF),
                dma((7,)), dma((PARTS,)), dma((PARTS,)), dma((PARTS,)),
                dma((ns - 1,)), dma((ns - 1,)), dma((1,)), dma((1,)),
                pltpu.SemaphoreType.REGULAR((2,)), pltpu.SemaphoreType.REGULAR((2,)),
            ],
            compiler_params=pltpu.CompilerParams(
                collective_id=0, has_side_effects=True, vmem_limit_bytes=40 * 1024 * 1024),
        )(*[pltpu.with_memory_space_constraint(a, pltpu.HBM) for a in operands])
        hbm = pl.BlockSpec(memory_space=pltpu.HBM)
        return pl.pallas_call(
            deliver,
            out_shape=[jax.ShapeDtypeStruct(a.shape, a.dtype) for a in outs],
            in_specs=[pl.BlockSpec(memory_space=pl.ANY)] * 2,
            out_specs=[hbm, hbm],
            scratch_shapes=[dma((2,))],
        )(*[pltpu.with_memory_space_constraint(a, vm) for a in outs])

    in_specs = (
        P("sweep", "recv", None), P(), P(), P(), P("recv"), P("recv"),
        P("sweep", None, None), P("sweep", "recv", None),
    )
    out_specs = (P("sweep", "recv", None), P("sweep", "recv", None))
    return jax.shard_map(local, mesh=mesh, in_specs=in_specs, out_specs=out_specs, check_vma=False)
```

```python
import functools
import math

import jax
import jax.numpy as jnp
from jax import lax
from jax.experimental import pallas as pl
from jax.experimental.pallas import tpu as pltpu
from jax.sharding import PartitionSpec as P

BF = jnp.bfloat16
F32 = jnp.float32
FINE = 32
LANES = 128
SIDES = 2
PARTS = 2
MESH = pl.DeviceIdType.MESH


def cube(nr):
    return (4, 8, 2) if nr == 64 else (1, nr // 2, 2)


def kernel(
    ns, nr,
    rec_h, pil_h, had_h, cv_h, own_h, live_h, fil_h, tgt_h,
    resp, grad,
    rec, pil, had, cv, own, live, fil, tgt,
    rect, wmat, xs, sb, rb, wgt, gs, ch, gb,
    in_sem, rec_sem, sib_send, sib_recv, s1_send, s1_recv, s2_send, s2_recv, pair, relay,
):
    me = lax.axis_index("sweep")
    mr = lax.axis_index("recv")
    _, held, half, samples = rec.shape
    chans = 2 * half
    codes, plen = pil.shape
    lags = fil.shape[1]
    owned = fil.shape[0]
    pairs = lags // FINE // 2
    rows = lags // nr
    nx, ny, nz = cube(nr)
    x, y, z = mr // (ny * nz), mr // nz % ny, mr % nz
    core = me % 2
    bits = (me // 4, me // 2 % 2, core)

    def mate(k):
        a, b, c = [1 - v if k >> (2 - i) & 1 else v for i, v in enumerate(bits)]
        return a * 4 + b * 2 + c

    def at(dx, dy, dz):
        return ((x + dx) % nx * ny + (y + dy) % ny) * nz + (z + dz) % nz

    sib = mate(1)
    order = [[6, 7, 4, 5], [2, 3, 1]]
    ranks = ns // SIDES
    slots = codes // SIDES

    barrier = pltpu.get_barrier_semaphore()
    ys = [{"recv": at(0, d, 0)} for d in sorted(range(1, ny), key=lambda d: -min(d, ny - d))]
    zs = [{"recv": at(0, 0, d)} for d in range(1, nz)]
    line = [{"recv": at(d, 0, 0)} for d in range(1, nx)]
    greet = zs + ys + [{"sweep": mate(k)} for k in (6, 4, 2)] + line

    def tell(sem, device):
        pl.semaphore_signal(sem, inc=1, device_id=device, device_id_type=MESH)

    @pl.when(core == 1)
    def _():
        tell(barrier, {"sweep": sib})

    part = samples // PARTS
    mine = pl.ds(pl.multiple_of(core * half, half), half)
    theirs = pl.ds(pl.multiple_of((1 - core) * half, half), half)
    small = [(pil_h, pil), (cv_h, cv), (had_h, had), (own_h, own), (live_h, live), (fil_h, fil), (tgt_h, tgt)]
    loads = [pltpu.make_async_copy(a, b, in_sem.at[i]) for i, (a, b) in enumerate(small)]
    own_rec = [
        pltpu.make_async_copy(
            rec_h.at[:, mine, pl.ds(i * part, part)], rec.at[0, :, :, pl.ds(i * part, part)], rec_sem.at[i])
        for i in range(PARTS)
    ]
    l_pil, l_cv, l_had, l_own, l_live, l_fil, l_tgt = loads
    l_pil.start()
    l_cv.start()
    for c in own_rec:
        c.start()
    for c in loads[2:]:
        c.start()

    @pl.when(core == 0)
    def _():
        pl.semaphore_wait(barrier, 1)
        tell(pair.at[0], {"sweep": sib})

    @pl.when(core == 1)
    def _():
        pl.semaphore_wait(pair.at[0], 1)
        for d in greet:
            tell(barrier, d)

    trade = [
        pltpu.make_async_remote_copy(
            src_ref=rec_h.at[:, theirs, pl.ds(i * part, part)],
            dst_ref=rec.at[1, :, :, pl.ds(i * part, part)],
            send_sem=sib_send.at[i], recv_sem=sib_recv.at[i],
            device_id={"sweep": sib}, device_id_type=MESH)
        for i in range(PARTS)
    ]
    for c in trade:
        c.start()

    l_pil.wait()
    l_cv.wait()
    slot_code = [owned * mate(k) + i for k in range(ns) for i in range(owned)]
    row = lax.broadcasted_iota(jnp.int32, (codes, codes), 0)
    col = lax.broadcasted_iota(jnp.int32, (codes, codes), 1)
    pick = jnp.zeros((codes, codes), jnp.int32)
    for q in range(codes):
        pick = jnp.where(row == q, cv[slot_code[q]], pick)
    onehot = (pick == col).astype(F32).astype(BF)
    cp = jnp.dot(onehot, pil[...], preferred_element_type=F32)
    cp = jnp.concatenate([cp, jnp.zeros((codes, samples - plen), F32)], axis=1)

    def build(g):
        own_slots = cp[g * slots:(g + 1) * slots]
        for f in range(0, FINE, 2):
            both = [pltpu.roll(own_slots, v, 1) if v else own_slots for v in (f, f + 1)]
            wmat[g, f * slots:(f + 2) * slots, :] = jnp.concatenate(both, axis=0).astype(BF)

    build(1)

    l_had.wait()

    rect[samples:samples + LANES, :] = jnp.zeros((LANES, LANES), BF)
    for i in range(PARTS):
        own_rec[i].wait()
        trade[i].wait_recv()
        for b in range(i * part // LANES, (i + 1) * part // LANES):
            blk = rec[:, :, :, b * LANES:(b + 1) * LANES].reshape(2 * held * half, LANES)
            rect[b * LANES:(b + 1) * LANES, :] = blk.T

    def copy1(k):
        return pltpu.make_async_remote_copy(
            src_ref=sb.at[k], dst_ref=rb.at[k - 1],
            send_sem=s1_send.at[k - 1], recv_sem=s1_recv.at[k - 1],
            device_id={"sweep": mate(k)}, device_id_type=MESH)

    lane = lax.broadcasted_iota(jnp.int32, (1, LANES), 1)
    group = lane // half
    norm = 1.0 / math.sqrt(codes)
    sweeps = [held * me + i for i in range(held)] + [held * sib + i for i in range(held)]
    coef = []
    for q in range(codes):
        v = jnp.zeros((1, LANES), F32)
        for g, s in enumerate(sweeps):
            v = jnp.where(group == g, had[s, slot_code[q]].astype(F32) * norm, v)
        coef.append(v)
    low = group < 2
    outer = (group == 0) | (group == 3)
    even = group % 2 == 0
    def correlate(g, p):
        base = 2 * FINE * p
        rhs = jnp.concatenate(
            [rect[base:base + samples, :], rect[base + FINE:base + FINE + samples, :]], axis=1)
        acc = jnp.dot(wmat[g], rhs, preferred_element_type=F32)
        xs[g, p, 0] = acc[:, :LANES]
        xs[g, p, 1] = acc[:, LANES:]

    def decode(g, p, k):
        q = owned * (k % ranks)
        a0, b0, a1, b1 = [
            xs[g, p, par, pl.ds(q + i, FINE, stride=slots), :] * coef[owned * k + i]
            for par in range(2) for i in range(owned)
        ]
        u = jnp.where(low, b0, b1) + pltpu.roll(jnp.where(low, b1, b0), 2 * half, 1)
        v = jnp.where(outer, a0, a1) + pltpu.roll(jnp.where(outer, a1, a0), 2 * half, 1)
        t = jnp.where(even, v, u) + pltpu.roll(jnp.where(even, u, v), half, 1)
        sb[k, p] = t.astype(BF)

    for g in (1, 0):
        for p in range(pairs):
            correlate(g, p)
            if g == 1 and p == 0:
                build(0)
            for k in range(g * ranks, (g + 1) * ranks):
                decode(g, p, k)
        if g == 1:
            @pl.when(core == 1)
            def _():
                pl.semaphore_wait(barrier, len(greet))
                tell(pair.at[1], {"sweep": sib})

            @pl.when(core == 0)
            def _():
                pl.semaphore_wait(pair.at[1], 1)

        for k in order[1 - g]:
            copy1(k).start()
        if g == 1:
            for d in ys:
                tell(relay.at[0], d)

    l_own.wait()
    l_live.wait()
    own_t = jnp.broadcast_to(own[...].astype(F32), (LANES, chans)).T
    live_t = jnp.broadcast_to(live[...].astype(F32), (LANES, chans)).T
    for c in range(owned):
        v = cv[owned * me + c].astype(F32)
        wgt[c * chans:(c + 1) * chans, :] = live_t * jnp.where(own_t == v, 1.25, 0.25)

    pl.semaphore_wait(relay.at[0], ny - 1)
    for d in line:
        tell(relay.at[1], d)

    first = jnp.full((FINE, LANES), core, jnp.int32) == 0
    pieces = []
    for ks in order:
        for k in ks:
            copy1(k).wait_recv()
    for p in range(pairs):
        here = sb[0, p].astype(F32)
        for k in (6, 4, 2):
            here = here + rb[k - 1, p].astype(F32)
        there = rb[6, p].astype(F32)
        for k in (5, 3, 1):
            there = there + rb[k - 1, p].astype(F32)
        h0 = jnp.where(first, here, there)
        h1 = jnp.where(first, there, here)
        pieces.append(jnp.where(low, h0, pltpu.roll(h1, 2 * half, 1)))
        pieces.append(jnp.where(low, pltpu.roll(h0, 2 * half, 1), h1))
    dec_t = jnp.concatenate(pieces, axis=0).astype(BF)
    dec = dec_t.T
    l_fil.wait()
    l_tgt.wait()
    res = []
    for c in range(owned):
        lhs = jnp.concatenate([dec[(h * owned + c) * half:(h * owned + c + 1) * half, :] for h in range(2)], axis=0)
        r = jnp.dot(lhs, fil[c], preferred_element_type=F32)
        resp[c] = r
        res.append((wgt[c * chans:(c + 1) * chans, :] * (r - tgt[c].astype(F32))).astype(BF))
    zero = jnp.zeros((half, lags), BF)
    blocks = []
    for h in range(2):
        for c in range(owned):
            blocks.append(jnp.concatenate(
                [res[c][h * half:(h + 1) * half, :] if e == c else zero for e in range(owned)], axis=1))
    g = jnp.dot(dec_t, jnp.concatenate(blocks, axis=0), preferred_element_type=F32)
    for c in range(owned):
        gs[c] = g[:, c * lags:(c + 1) * lags]
    ch[...] = jnp.stack(
        [gs[c, pl.ds(i, nr, stride=rows), :] for c in range(owned) for i in range(rows)], axis=1).astype(BF)

    steps = [(dx, dy, dz) for dx in range(nx) for dy in range(ny) for dz in range(nz)]
    steps.sort(key=lambda s: -(min(s[0], nx - s[0]) + min(s[1], ny - s[1]) + 4 * s[2]))
    pl.semaphore_wait(relay.at[1], nx - 1)
    for n, s in enumerate(steps[:-1]):
        j = at(*s)
        pltpu.make_async_remote_copy(
            src_ref=ch.at[j], dst_ref=gb.at[n], send_sem=s2_send.at[0], recv_sem=s2_recv.at[0],
            device_id={"recv": j}, device_id_type=MESH).start()

    total = ch[mr].astype(F32)
    for c in trade:
        c.wait_send()
    for ks in order:
        for k in ks:
            copy1(k).wait_send()
    sent = ch.at[pl.ds(0, nr - 1)]
    pltpu.make_async_copy(sent, sent, s2_send.at[0]).wait()
    pltpu.make_async_copy(gb, gb, s2_recv.at[0]).wait()
    total = total + jnp.sum(gb[...].astype(F32), axis=0)
    factor = 1.0 / math.sqrt(chans * nr)
    for c in range(owned):
        grad[c] = total[c * rows:(c + 1) * rows, :] * factor


def deliver(resp_v, grad_v, resp_h, grad_h, sem):
    outs = [pltpu.make_async_copy(resp_v, resp_h, sem.at[0]), pltpu.make_async_copy(grad_v, grad_h, sem.at[1])]
    for c in outs:
        c.start()
    for c in outs:
        c.wait()


def solution(mesh):
    ns, nr = mesh.shape["sweep"], mesh.shape["recv"]

    def local(records, pilots, hadamard, code_vibrator, owner_map, live_mask, filters, targets):
        held, chans, samples = records.shape
        codes, plen = pilots.shape
        owned, lags, _ = filters.shape
        rows = lags // nr
        pairs = lags // FINE // 2
        vm = pltpu.VMEM
        dma = pltpu.SemaphoreType.DMA
        operands = (records, pilots, hadamard, code_vibrator, owner_map.reshape(1, -1),
                    live_mask.reshape(1, -1), filters, targets)
        outs = pl.pallas_call(
            functools.partial(kernel, ns, nr),
            out_shape=(vm((owned, chans, lags), F32), vm((owned, rows, lags), F32)),
            in_specs=[pl.BlockSpec(memory_space=pltpu.HBM)] * 8,
            out_specs=(pl.BlockSpec(memory_space=vm),) * 2,
            scratch_shapes=[
                vm((2, held, chans // 2, samples), BF), vm((codes, plen), BF),
                pltpu.SMEM((codes, codes), jnp.int32), pltpu.SMEM((codes,), jnp.int32),
                vm((1, chans), jnp.int32), vm((1, chans), jnp.int32),
                vm((owned, lags, lags), BF), vm((owned, chans, lags), BF),
                vm((samples + LANES, LANES), BF), vm((SIDES, FINE * codes // SIDES, samples), BF),
                vm((SIDES, pairs, 2, FINE * codes // SIDES, LANES), F32),
                vm((ns, pairs, FINE, LANES), BF), vm((ns - 1, pairs, FINE, LANES), BF),
                vm((owned * chans, lags), F32), vm((owned, lags, lags), F32),
                vm((nr, owned * rows, lags), BF), vm((nr - 1, owned * rows, lags), BF),
                dma((7,)), dma((PARTS,)), dma((PARTS,)), dma((PARTS,)),
                dma((ns - 1,)), dma((ns - 1,)), dma((1,)), dma((1,)),
                pltpu.SemaphoreType.REGULAR((2,)), pltpu.SemaphoreType.REGULAR((2,)),
            ],
            compiler_params=pltpu.CompilerParams(
                collective_id=0, has_side_effects=True, vmem_limit_bytes=40 * 1024 * 1024),
        )(*[pltpu.with_memory_space_constraint(a, pltpu.HBM) for a in operands])
        hbm = pl.BlockSpec(memory_space=pltpu.HBM)
        return pl.pallas_call(
            deliver,
            out_shape=[jax.ShapeDtypeStruct(a.shape, a.dtype) for a in outs],
            in_specs=[pl.BlockSpec(memory_space=pl.ANY)] * 2,
            out_specs=[hbm, hbm],
            scratch_shapes=[dma((2,))],
        )(*[pltpu.with_memory_space_constraint(a, vm) for a in outs])

    in_specs = (
        P("sweep", "recv", None), P(), P(), P(), P("recv"), P("recv"),
        P("sweep", None, None), P("sweep", "recv", None),
    )
    out_specs = (P("sweep", "recv", None), P("sweep", "recv", None))
    return jax.shard_map(local, mesh=mesh, in_specs=in_specs, out_specs=out_specs, check_vma=False)
```

```python
import functools
import math

import jax
import jax.numpy as jnp
from jax import lax
from jax.experimental import pallas as pl
from jax.experimental.pallas import tpu as pltpu
from jax.sharding import PartitionSpec as P

BF = jnp.bfloat16
F32 = jnp.float32
FINE = 32
LANES = 128
SIDES = 2
PARTS = 2
MESH = pl.DeviceIdType.MESH


def cube(nr):
    return (4, 8, 2) if nr == 64 else (1, nr // 2, 2)


def kernel(
    ns, nr,
    rec_h, pil_h, had_h, cv_h, own_h, live_h, fil_h, tgt_h,
    resp, grad,
    rec, pil, had, cv, own, live, fil, tgt,
    rect, wmat, xs, sb, rb, wgt, gs, ch, gb,
    in_sem, rec_sem, sib_send, sib_recv, s1_send, s1_recv, s2_send, s2_recv, pair, relay,
):
    me = lax.axis_index("sweep")
    mr = lax.axis_index("recv")
    _, held, half, samples = rec.shape
    chans = 2 * half
    codes, plen = pil.shape
    lags = fil.shape[1]
    owned = fil.shape[0]
    pairs = lags // FINE // 2
    rows = lags // nr
    nx, ny, nz = cube(nr)
    x, y, z = mr // (ny * nz), mr // nz % ny, mr % nz
    core = me % 2
    bits = (me // 4, me // 2 % 2, core)

    def mate(k):
        a, b, c = [1 - v if k >> (2 - i) & 1 else v for i, v in enumerate(bits)]
        return a * 4 + b * 2 + c

    def at(dx, dy, dz):
        return ((x + dx) % nx * ny + (y + dy) % ny) * nz + (z + dz) % nz

    sib = mate(1)
    order = [[7, 6, 5, 4], [3, 2, 1]]
    ranks = ns // SIDES
    slots = codes // SIDES

    barrier = pltpu.get_barrier_semaphore()
    ys = [{"recv": at(0, d, 0)} for d in sorted(range(1, ny), key=lambda d: -min(d, ny - d))]
    zs = [{"recv": at(0, 0, d)} for d in range(1, nz)]
    line = [{"recv": at(d, 0, 0)} for d in range(1, nx)]
    greet = zs + ys + [{"sweep": mate(k)} for k in (6, 4, 2)] + line

    def tell(sem, device):
        pl.semaphore_signal(sem, inc=1, device_id=device, device_id_type=MESH)

    @pl.when(core == 1)
    def _():
        tell(barrier, {"sweep": sib})

    part = samples // PARTS
    mine = pl.ds(pl.multiple_of(core * half, half), half)
    theirs = pl.ds(pl.multiple_of((1 - core) * half, half), half)
    small = [(pil_h, pil), (cv_h, cv), (had_h, had), (own_h, own), (live_h, live), (fil_h, fil), (tgt_h, tgt)]
    loads = [pltpu.make_async_copy(a, b, in_sem.at[i]) for i, (a, b) in enumerate(small)]
    own_rec = [
        pltpu.make_async_copy(
            rec_h.at[:, mine, pl.ds(i * part, part)], rec.at[0, :, :, pl.ds(i * part, part)], rec_sem.at[i])
        for i in range(PARTS)
    ]
    l_pil, l_cv, l_had, l_own, l_live, l_fil, l_tgt = loads
    l_pil.start()
    l_cv.start()
    for c in own_rec:
        c.start()
    for c in loads[2:]:
        c.start()

    @pl.when(core == 0)
    def _():
        pl.semaphore_wait(barrier, 1)
        tell(pair.at[0], {"sweep": sib})

    @pl.when(core == 1)
    def _():
        pl.semaphore_wait(pair.at[0], 1)
        for d in greet:
            tell(barrier, d)

    trade = [
        pltpu.make_async_remote_copy(
            src_ref=rec_h.at[:, theirs, pl.ds(i * part, part)],
            dst_ref=rec.at[1, :, :, pl.ds(i * part, part)],
            send_sem=sib_send.at[i], recv_sem=sib_recv.at[i],
            device_id={"sweep": sib}, device_id_type=MESH)
        for i in range(PARTS)
    ]
    for c in trade:
        c.start()

    l_pil.wait()
    l_cv.wait()
    slot_code = [owned * mate(k) + i for k in range(ns) for i in range(owned)]
    row = lax.broadcasted_iota(jnp.int32, (codes, codes), 0)
    col = lax.broadcasted_iota(jnp.int32, (codes, codes), 1)
    pick = jnp.zeros((codes, codes), jnp.int32)
    for q in range(codes):
        pick = jnp.where(row == q, cv[slot_code[q]], pick)
    onehot = (pick == col).astype(F32).astype(BF)
    cp = jnp.dot(onehot, pil[...], preferred_element_type=F32)
    cp = jnp.concatenate([cp, jnp.zeros((codes, samples - plen), F32)], axis=1)

    def build(g):
        own_slots = cp[g * slots:(g + 1) * slots]
        for f in range(0, FINE, 2):
            both = [pltpu.roll(own_slots, v, 1) if v else own_slots for v in (f, f + 1)]
            wmat[g, f * slots:(f + 2) * slots, :] = jnp.concatenate(both, axis=0).astype(BF)

    build(1)

    l_had.wait()

    rect[samples:samples + LANES, :] = jnp.zeros((LANES, LANES), BF)
    for i in range(PARTS):
        own_rec[i].wait()
        trade[i].wait_recv()
        for b in range(i * part // LANES, (i + 1) * part // LANES):
            blk = rec[:, :, :, b * LANES:(b + 1) * LANES].reshape(2 * held * half, LANES)
            rect[b * LANES:(b + 1) * LANES, :] = blk.T

    def copy1(k):
        return pltpu.make_async_remote_copy(
            src_ref=sb.at[k], dst_ref=rb.at[k - 1],
            send_sem=s1_send.at[k - 1], recv_sem=s1_recv.at[k - 1],
            device_id={"sweep": mate(k)}, device_id_type=MESH)

    lane = lax.broadcasted_iota(jnp.int32, (1, LANES), 1)
    group = lane // half
    norm = 1.0 / math.sqrt(codes)
    sweeps = [held * me + i for i in range(held)] + [held * sib + i for i in range(held)]
    coef = []
    for q in range(codes):
        v = jnp.zeros((1, LANES), F32)
        for g, s in enumerate(sweeps):
            v = jnp.where(group == g, had[s, slot_code[q]].astype(F32) * norm, v)
        coef.append(v)
    low = group < 2
    outer = (group == 0) | (group == 3)
    even = group % 2 == 0
    def correlate(g):
        rhs = jnp.concatenate([rect[n * FINE:n * FINE + samples, :] for n in range(2 * pairs)], axis=1)
        acc = jnp.dot(wmat[g], rhs, preferred_element_type=F32)
        for n in range(2 * pairs):
            xs[g, n // 2, n % 2] = acc[:, n * LANES:(n + 1) * LANES]

    def decode(g, p, k):
        q = owned * (k % ranks)
        a0, b0, a1, b1 = [
            xs[g, p, par, pl.ds(q + i, FINE, stride=slots), :] * coef[owned * k + i]
            for par in range(2) for i in range(owned)
        ]
        u = jnp.where(low, b0, b1) + pltpu.roll(jnp.where(low, b1, b0), 2 * half, 1)
        v = jnp.where(outer, a0, a1) + pltpu.roll(jnp.where(outer, a1, a0), 2 * half, 1)
        t = jnp.where(even, v, u) + pltpu.roll(jnp.where(even, u, v), half, 1)
        sb[k, p] = t.astype(BF)

    for g in (1, 0):
        correlate(g)
        if g == 1:
            build(0)
        for p in range(pairs):
            for k in range(g * ranks, (g + 1) * ranks):
                decode(g, p, k)
        if g == 1:
            @pl.when(core == 1)
            def _():
                pl.semaphore_wait(barrier, len(greet))
                tell(pair.at[1], {"sweep": sib})

            @pl.when(core == 0)
            def _():
                pl.semaphore_wait(pair.at[1], 1)

        for k in order[1 - g]:
            copy1(k).start()
        if g == 1:
            for d in ys:
                tell(relay.at[0], d)

    l_own.wait()
    l_live.wait()
    own_t = jnp.broadcast_to(own[...].astype(F32), (LANES, chans)).T
    live_t = jnp.broadcast_to(live[...].astype(F32), (LANES, chans)).T
    for c in range(owned):
        v = cv[owned * me + c].astype(F32)
        wgt[c * chans:(c + 1) * chans, :] = live_t * jnp.where(own_t == v, 1.25, 0.25)

    pl.semaphore_wait(relay.at[0], ny - 1)
    for d in line:
        tell(relay.at[1], d)

    first = jnp.full((FINE, LANES), core, jnp.int32) == 0
    pieces = []
    l_fil.wait()
    l_tgt.wait()
    for k in (1, 2, 3):
        copy1(k).wait_recv()
    sums = [(sb[0, p].astype(F32) + rb[1, p].astype(F32), rb[0, p].astype(F32) + rb[2, p].astype(F32))
            for p in range(pairs)]
    for k in order[0]:
        copy1(k).wait_recv()
    for p in range(pairs):
        here, there = sums[p]
        for k in (4, 6):
            here = here + rb[k - 1, p].astype(F32)
            there = there + rb[k, p].astype(F32)
        h0 = jnp.where(first, here, there)
        h1 = jnp.where(first, there, here)
        pieces.append(jnp.where(low, h0, pltpu.roll(h1, 2 * half, 1)))
        pieces.append(jnp.where(low, pltpu.roll(h0, 2 * half, 1), h1))
    dec_t = jnp.concatenate(pieces, axis=0).astype(BF)
    dec = dec_t.T
    res = []
    for c in range(owned):
        lhs = jnp.concatenate([dec[(h * owned + c) * half:(h * owned + c + 1) * half, :] for h in range(2)], axis=0)
        r = jnp.dot(lhs, fil[c], preferred_element_type=F32)
        resp[c] = r
        res.append((wgt[c * chans:(c + 1) * chans, :] * (r - tgt[c].astype(F32))).astype(BF))
    zero = jnp.zeros((half, lags), BF)
    blocks = []
    for h in range(2):
        for c in range(owned):
            blocks.append(jnp.concatenate(
                [res[c][h * half:(h + 1) * half, :] if e == c else zero for e in range(owned)], axis=1))
    g = jnp.dot(dec_t, jnp.concatenate(blocks, axis=0), preferred_element_type=F32)
    for c in range(owned):
        gs[c] = g[:, c * lags:(c + 1) * lags]
    ch[...] = jnp.stack(
        [gs[c, pl.ds(i, nr, stride=rows), :] for c in range(owned) for i in range(rows)], axis=1).astype(BF)

    steps = [(dx, dy, dz) for dx in range(nx) for dy in range(ny) for dz in range(nz)]
    steps.sort(key=lambda s: -(min(s[0], nx - s[0]) + min(s[1], ny - s[1]) + 4 * s[2]))
    pl.semaphore_wait(relay.at[1], nx - 1)
    for n, s in enumerate(steps[:-1]):
        j = at(*s)
        pltpu.make_async_remote_copy(
            src_ref=ch.at[j], dst_ref=gb.at[n], send_sem=s2_send.at[0], recv_sem=s2_recv.at[0],
            device_id={"recv": j}, device_id_type=MESH).start()

    total = ch[mr].astype(F32)
    for c in trade:
        c.wait_send()
    for ks in order:
        for k in ks:
            copy1(k).wait_send()
    sent = ch.at[pl.ds(0, nr - 1)]
    pltpu.make_async_copy(sent, sent, s2_send.at[0]).wait()
    pltpu.make_async_copy(gb, gb, s2_recv.at[0]).wait()
    total = total + jnp.sum(gb[...].astype(F32), axis=0)
    factor = 1.0 / math.sqrt(chans * nr)
    for c in range(owned):
        grad[c] = total[c * rows:(c + 1) * rows, :] * factor


def deliver(resp_v, grad_v, resp_h, grad_h, sem):
    outs = [pltpu.make_async_copy(resp_v, resp_h, sem.at[0]), pltpu.make_async_copy(grad_v, grad_h, sem.at[1])]
    for c in outs:
        c.start()
    for c in outs:
        c.wait()


def solution(mesh):
    ns, nr = mesh.shape["sweep"], mesh.shape["recv"]

    def local(records, pilots, hadamard, code_vibrator, owner_map, live_mask, filters, targets):
        held, chans, samples = records.shape
        codes, plen = pilots.shape
        owned, lags, _ = filters.shape
        rows = lags // nr
        pairs = lags // FINE // 2
        vm = pltpu.VMEM
        dma = pltpu.SemaphoreType.DMA
        operands = (records, pilots, hadamard, code_vibrator, owner_map.reshape(1, -1),
                    live_mask.reshape(1, -1), filters, targets)
        outs = pl.pallas_call(
            functools.partial(kernel, ns, nr),
            out_shape=(vm((owned, chans, lags), F32), vm((owned, rows, lags), F32)),
            in_specs=[pl.BlockSpec(memory_space=pltpu.HBM)] * 8,
            out_specs=(pl.BlockSpec(memory_space=vm),) * 2,
            scratch_shapes=[
                vm((2, held, chans // 2, samples), BF), vm((codes, plen), BF),
                pltpu.SMEM((codes, codes), jnp.int32), pltpu.SMEM((codes,), jnp.int32),
                vm((1, chans), jnp.int32), vm((1, chans), jnp.int32),
                vm((owned, lags, lags), BF), vm((owned, chans, lags), BF),
                vm((samples + LANES, LANES), BF), vm((SIDES, FINE * codes // SIDES, samples), BF),
                vm((SIDES, pairs, 2, FINE * codes // SIDES, LANES), F32),
                vm((ns, pairs, FINE, LANES), BF), vm((ns - 1, pairs, FINE, LANES), BF),
                vm((owned * chans, lags), F32), vm((owned, lags, lags), F32),
                vm((nr, owned * rows, lags), BF), vm((nr - 1, owned * rows, lags), BF),
                dma((7,)), dma((PARTS,)), dma((PARTS,)), dma((PARTS,)),
                dma((ns - 1,)), dma((ns - 1,)), dma((1,)), dma((1,)),
                pltpu.SemaphoreType.REGULAR((2,)), pltpu.SemaphoreType.REGULAR((2,)),
            ],
            compiler_params=pltpu.CompilerParams(
                collective_id=0, has_side_effects=True, vmem_limit_bytes=40 * 1024 * 1024),
        )(*[pltpu.with_memory_space_constraint(a, pltpu.HBM) for a in operands])
        hbm = pl.BlockSpec(memory_space=pltpu.HBM)
        return pl.pallas_call(
            deliver,
            out_shape=[jax.ShapeDtypeStruct(a.shape, a.dtype) for a in outs],
            in_specs=[pl.BlockSpec(memory_space=pl.ANY)] * 2,
            out_specs=[hbm, hbm],
            scratch_shapes=[dma((2,))],
        )(*[pltpu.with_memory_space_constraint(a, vm) for a in outs])

    in_specs = (
        P("sweep", "recv", None), P(), P(), P(), P("recv"), P("recv"),
        P("sweep", None, None), P("sweep", "recv", None),
    )
    out_specs = (P("sweep", "recv", None), P("sweep", "recv", None))
    return jax.shard_map(local, mesh=mesh, in_specs=in_specs, out_specs=out_specs, check_vma=False)
```

```python
import functools
import math

import jax
import jax.numpy as jnp
from jax import lax
from jax.experimental import pallas as pl
from jax.experimental.pallas import tpu as pltpu
from jax.sharding import PartitionSpec as P

BF = jnp.bfloat16
F32 = jnp.float32
FINE = 32
LANES = 128
SIDES = 2
PARTS = 2
MESH = pl.DeviceIdType.MESH


def cube(nr):
    return (4, 8, 2) if nr == 64 else (1, nr // 2, 2)


def kernel(
    ns, nr,
    rec_h, pil_h, had_h, cv_h, own_h, live_h, fil_h, tgt_h,
    resp, grad,
    rec, pil, had, cv, own, live, fil, tgt,
    rect, wmat, xs, sb, rb, wgt, gs, ch, gb,
    in_sem, rec_sem, sib_send, sib_recv, s1_send, s1_recv, s2_send, s2_recv, pair, relay,
):
    me = lax.axis_index("sweep")
    mr = lax.axis_index("recv")
    _, held, half, samples = rec.shape
    chans = 2 * half
    codes, plen = pil.shape
    lags = fil.shape[1]
    owned = fil.shape[0]
    pairs = lags // FINE // 2
    rows = lags // nr
    nx, ny, nz = cube(nr)
    x, y, z = mr // (ny * nz), mr // nz % ny, mr % nz
    core = me % 2
    bits = (me // 4, me // 2 % 2, core)

    def mate(k):
        a, b, c = [1 - v if k >> (2 - i) & 1 else v for i, v in enumerate(bits)]
        return a * 4 + b * 2 + c

    def at(dx, dy, dz):
        return ((x + dx) % nx * ny + (y + dy) % ny) * nz + (z + dz) % nz

    sib = mate(1)
    order = [[7, 6, 5, 4], [3, 2, 1]]
    ranks = ns // SIDES
    slots = codes // SIDES

    barrier = pltpu.get_barrier_semaphore()
    ys = [{"recv": at(0, d, 0)} for d in sorted(range(1, ny), key=lambda d: -min(d, ny - d))]
    zs = [{"recv": at(0, 0, d)} for d in range(1, nz)]
    line = [{"recv": at(d, 0, 0)} for d in range(1, nx)]
    greet = zs + ys + [{"sweep": mate(k)} for k in (6, 4, 2)] + line

    def tell(sem, device):
        pl.semaphore_signal(sem, inc=1, device_id=device, device_id_type=MESH)

    @pl.when(core == 1)
    def _():
        tell(barrier, {"sweep": sib})

    part = samples // PARTS
    mine = pl.ds(pl.multiple_of(core * half, half), half)
    theirs = pl.ds(pl.multiple_of((1 - core) * half, half), half)
    small = [(pil_h, pil), (cv_h, cv), (had_h, had), (own_h, own), (live_h, live), (fil_h, fil), (tgt_h, tgt)]
    loads = [pltpu.make_async_copy(a, b, in_sem.at[i]) for i, (a, b) in enumerate(small)]
    own_rec = [
        pltpu.make_async_copy(
            rec_h.at[:, mine, pl.ds(i * part, part)], rec.at[0, :, :, pl.ds(i * part, part)], rec_sem.at[i])
        for i in range(PARTS)
    ]
    l_pil, l_cv, l_had, l_own, l_live, l_fil, l_tgt = loads
    l_pil.start()
    l_cv.start()
    for c in own_rec:
        c.start()
    for c in loads[2:]:
        c.start()

    @pl.when(core == 0)
    def _():
        pl.semaphore_wait(barrier, 1)
        tell(pair.at[0], {"sweep": sib})

    @pl.when(core == 1)
    def _():
        pl.semaphore_wait(pair.at[0], 1)
        for d in greet:
            tell(barrier, d)

    trade = [
        pltpu.make_async_remote_copy(
            src_ref=rec_h.at[:, theirs, pl.ds(i * part, part)],
            dst_ref=rec.at[1, :, :, pl.ds(i * part, part)],
            send_sem=sib_send.at[i], recv_sem=sib_recv.at[i],
            device_id={"sweep": sib}, device_id_type=MESH)
        for i in range(PARTS)
    ]
    for c in trade:
        c.start()

    l_pil.wait()
    l_cv.wait()
    slot_code = [owned * mate(k) + i for k in range(ns) for i in range(owned)]
    row = lax.broadcasted_iota(jnp.int32, (codes, codes), 0)
    col = lax.broadcasted_iota(jnp.int32, (codes, codes), 1)
    pick = jnp.zeros((codes, codes), jnp.int32)
    for q in range(codes):
        pick = jnp.where(row == q, cv[slot_code[q]], pick)
    onehot = (pick == col).astype(F32).astype(BF)
    cp = jnp.dot(onehot, pil[...], preferred_element_type=F32)
    cp = jnp.concatenate([cp, jnp.zeros((codes, samples - plen), F32)], axis=1)

    def build(g):
        own_slots = cp[g * slots:(g + 1) * slots]
        for f in range(0, FINE, 2):
            both = [pltpu.roll(own_slots, v, 1) if v else own_slots for v in (f, f + 1)]
            wmat[g, f * slots:(f + 2) * slots, :] = jnp.concatenate(both, axis=0).astype(BF)

    build(1)

    l_had.wait()

    rect[samples:samples + LANES, :] = jnp.zeros((LANES, LANES), BF)
    for i in range(PARTS):
        own_rec[i].wait()
        trade[i].wait_recv()
        for b in range(i * part // LANES, (i + 1) * part // LANES):
            blk = rec[:, :, :, b * LANES:(b + 1) * LANES].reshape(2 * held * half, LANES)
            rect[b * LANES:(b + 1) * LANES, :] = blk.T

    def copy1(k):
        return pltpu.make_async_remote_copy(
            src_ref=sb.at[k], dst_ref=rb.at[k - 1],
            send_sem=s1_send.at[k - 1], recv_sem=s1_recv.at[k - 1],
            device_id={"sweep": mate(k)}, device_id_type=MESH)

    lane = lax.broadcasted_iota(jnp.int32, (1, LANES), 1)
    group = lane // half
    norm = 1.0 / math.sqrt(codes)
    sweeps = [held * me + i for i in range(held)] + [held * sib + i for i in range(held)]
    coef = []
    for q in range(codes):
        v = jnp.zeros((1, LANES), F32)
        for g, s in enumerate(sweeps):
            v = jnp.where(group == g, had[s, slot_code[q]].astype(F32) * norm, v)
        coef.append(v)
    low = group < 2
    outer = (group == 0) | (group == 3)
    even = group % 2 == 0
    def correlate(g):
        rhs = jnp.concatenate([rect[n * FINE:n * FINE + samples, :] for n in range(2 * pairs)], axis=1)
        acc = jnp.dot(wmat[g], rhs, preferred_element_type=F32)
        for n in range(2 * pairs):
            xs[g, n // 2, n % 2] = acc[:, n * LANES:(n + 1) * LANES]

    def decode(g, p, k):
        q = owned * (k % ranks)
        a0, b0, a1, b1 = [
            xs[g, p, par, pl.ds(q + i, FINE, stride=slots), :] * coef[owned * k + i]
            for par in range(2) for i in range(owned)
        ]
        u = jnp.where(low, b0, b1) + pltpu.roll(jnp.where(low, b1, b0), 2 * half, 1)
        v = jnp.where(outer, a0, a1) + pltpu.roll(jnp.where(outer, a1, a0), 2 * half, 1)
        t = jnp.where(even, v, u) + pltpu.roll(jnp.where(even, u, v), half, 1)
        sb[k, p] = t.astype(BF)

    for g in (1, 0):
        correlate(g)
        if g == 1:
            build(0)
        for p in range(pairs):
            for k in range(g * ranks, (g + 1) * ranks):
                decode(g, p, k)
        if g == 1:
            @pl.when(core == 1)
            def _():
                pl.semaphore_wait(barrier, len(greet))
                tell(pair.at[1], {"sweep": sib})

            @pl.when(core == 0)
            def _():
                pl.semaphore_wait(pair.at[1], 1)

        for k in order[1 - g]:
            copy1(k).start()
        if g == 1:
            for d in ys:
                tell(relay.at[0], d)

    l_own.wait()
    l_live.wait()
    own_t = jnp.broadcast_to(own[...].astype(F32), (LANES, chans)).T
    live_t = jnp.broadcast_to(live[...].astype(F32), (LANES, chans)).T
    for c in range(owned):
        v = cv[owned * me + c].astype(F32)
        wgt[c * chans:(c + 1) * chans, :] = live_t * jnp.where(own_t == v, 1.25, 0.25)

    pl.semaphore_wait(relay.at[0], ny - 1)
    for d in line:
        tell(relay.at[1], d)

    first = jnp.full((FINE, LANES), core, jnp.int32) == 0
    pieces = []
    l_fil.wait()
    l_tgt.wait()
    for k in (1, 2, 3):
        copy1(k).wait_recv()
    sums = [(sb[0, p].astype(F32) + rb[1, p].astype(F32), rb[0, p].astype(F32) + rb[2, p].astype(F32))
            for p in range(pairs)]
    for k in order[0]:
        copy1(k).wait_recv()
    for p in range(pairs):
        here, there = sums[p]
        for k in (4, 6):
            here = here + rb[k - 1, p].astype(F32)
            there = there + rb[k, p].astype(F32)
        h0 = jnp.where(first, here, there)
        h1 = jnp.where(first, there, here)
        pieces.append(jnp.where(low, h0, pltpu.roll(h1, 2 * half, 1)))
        pieces.append(jnp.where(low, pltpu.roll(h0, 2 * half, 1), h1))
    dec_t = jnp.concatenate(pieces, axis=0).astype(BF)
    dec = dec_t.T
    res = []
    for c in range(owned):
        lhs = jnp.concatenate([dec[(h * owned + c) * half:(h * owned + c + 1) * half, :] for h in range(2)], axis=0)
        r = jnp.dot(lhs, fil[c], preferred_element_type=F32)
        resp[c] = r
        res.append((wgt[c * chans:(c + 1) * chans, :] * (r - tgt[c].astype(F32))).astype(BF))
    zero = jnp.zeros((half, lags), BF)
    blocks = []
    for h in range(2):
        for c in range(owned):
            blocks.append(jnp.concatenate(
                [res[c][h * half:(h + 1) * half, :] if e == c else zero for e in range(owned)], axis=1))
    g = jnp.dot(dec_t, jnp.concatenate(blocks, axis=0), preferred_element_type=F32)
    for c in range(owned):
        gs[c] = g[:, c * lags:(c + 1) * lags]
    ch[...] = jnp.stack(
        [gs[c, pl.ds(i, nr, stride=rows), :] for c in range(owned) for i in range(rows)], axis=1).astype(BF)

    def outward(i, n):
        return n // 2 + (i + 1) // 2 * (1 - 2 * (i % 2))

    pl.semaphore_wait(relay.at[1], nx - 1)
    @pl.loop(0, nr - 1)
    def _(n):
        j = at(outward(n % nx, nx), outward(n // nx % ny, ny), nz - 1 - n // (nx * ny))
        pltpu.make_async_remote_copy(
            src_ref=ch.at[j], dst_ref=gb.at[n], send_sem=s2_send.at[0], recv_sem=s2_recv.at[0],
            device_id={"recv": j}, device_id_type=MESH).start()

    total = ch[mr].astype(F32)
    for c in trade:
        c.wait_send()
    for ks in order:
        for k in ks:
            copy1(k).wait_send()
    sent = ch.at[pl.ds(0, nr - 1)]
    pltpu.make_async_copy(sent, sent, s2_send.at[0]).wait()
    pltpu.make_async_copy(gb, gb, s2_recv.at[0]).wait()
    total = total + jnp.sum(gb[...].astype(F32), axis=0)
    factor = 1.0 / math.sqrt(chans * nr)
    for c in range(owned):
        grad[c] = total[c * rows:(c + 1) * rows, :] * factor


def deliver(resp_v, grad_v, resp_h, grad_h, sem):
    outs = [pltpu.make_async_copy(resp_v, resp_h, sem.at[0]), pltpu.make_async_copy(grad_v, grad_h, sem.at[1])]
    for c in outs:
        c.start()
    for c in outs:
        c.wait()


def solution(mesh):
    ns, nr = mesh.shape["sweep"], mesh.shape["recv"]

    def local(records, pilots, hadamard, code_vibrator, owner_map, live_mask, filters, targets):
        held, chans, samples = records.shape
        codes, plen = pilots.shape
        owned, lags, _ = filters.shape
        rows = lags // nr
        pairs = lags // FINE // 2
        vm = pltpu.VMEM
        dma = pltpu.SemaphoreType.DMA
        operands = (records, pilots, hadamard, code_vibrator, owner_map.reshape(1, -1),
                    live_mask.reshape(1, -1), filters, targets)
        outs = pl.pallas_call(
            functools.partial(kernel, ns, nr),
            out_shape=(vm((owned, chans, lags), F32), vm((owned, rows, lags), F32)),
            in_specs=[pl.BlockSpec(memory_space=pltpu.HBM)] * 8,
            out_specs=(pl.BlockSpec(memory_space=vm),) * 2,
            scratch_shapes=[
                vm((2, held, chans // 2, samples), BF), vm((codes, plen), BF),
                pltpu.SMEM((codes, codes), jnp.int32), pltpu.SMEM((codes,), jnp.int32),
                vm((1, chans), jnp.int32), vm((1, chans), jnp.int32),
                vm((owned, lags, lags), BF), vm((owned, chans, lags), BF),
                vm((samples + LANES, LANES), BF), vm((SIDES, FINE * codes // SIDES, samples), BF),
                vm((SIDES, pairs, 2, FINE * codes // SIDES, LANES), F32),
                vm((ns, pairs, FINE, LANES), BF), vm((ns - 1, pairs, FINE, LANES), BF),
                vm((owned * chans, lags), F32), vm((owned, lags, lags), F32),
                vm((nr, owned * rows, lags), BF), vm((nr - 1, owned * rows, lags), BF),
                dma((7,)), dma((PARTS,)), dma((PARTS,)), dma((PARTS,)),
                dma((ns - 1,)), dma((ns - 1,)), dma((1,)), dma((1,)),
                pltpu.SemaphoreType.REGULAR((2,)), pltpu.SemaphoreType.REGULAR((2,)),
            ],
            compiler_params=pltpu.CompilerParams(
                collective_id=0, has_side_effects=True, vmem_limit_bytes=40 * 1024 * 1024),
        )(*[pltpu.with_memory_space_constraint(a, pltpu.HBM) for a in operands])
        hbm = pl.BlockSpec(memory_space=pltpu.HBM)
        return pl.pallas_call(
            deliver,
            out_shape=[jax.ShapeDtypeStruct(a.shape, a.dtype) for a in outs],
            in_specs=[pl.BlockSpec(memory_space=pl.ANY)] * 2,
            out_specs=[hbm, hbm],
            scratch_shapes=[dma((2,))],
        )(*[pltpu.with_memory_space_constraint(a, vm) for a in outs])

    in_specs = (
        P("sweep", "recv", None), P(), P(), P(), P("recv"), P("recv"),
        P("sweep", None, None), P("sweep", "recv", None),
    )
    out_specs = (P("sweep", "recv", None), P("sweep", "recv", None))
    return jax.shard_map(local, mesh=mesh, in_specs=in_specs, out_specs=out_specs, check_vma=False)
```
